32 devices in a mesh: dim: 2 (over core), grp: 16 (over z, y, x).
Axes of the slice: x: 2, y: 2, z: 4, core: 2. Of those that a mesh axis runs over, the one named last changes fastest.
Arguments:
- states: bfloat16 [32768, 4096], P('grp', 'dim'), may hold values from -6 to 6
- pca: bfloat16 [4096, 1024], P('dim'), may hold values from -0.125 to 0.125
- centroids: float32 [256, 1024], P(None, 'dim'), may hold values from -3 to 3
- list_ids: int32 [32768, 1], P('grp'), may hold values from 0 to 255; in each aligned block of 2048 rows (0 to 2047, 2048 to 4095, ...) at most 16 rows name the same one
- prior_counts: int32 [256], P('grp'), may hold values from 1 to 63
- prior_gram: float32 [256, 1024, 1024], P('grp', 'dim'), may hold values from -96 to 96
Outputs:
- moments: float32 [256, 1024, 1024], P('grp', 'dim')
The draws below stay inside these ranges and needn't reach their ends.
Inputs may be any that keep to these rules, and one draw needn't show every extreme that they name: `list_ids`: among the passages of one index of grp, no list is named by more than 16 passages, a bound that some block reaches.
All inputs are finite; a program needn't handle non-finite values.
Results may differ from the reference program's by a relative error of at most 0.0095.
Values may be sent and summed in bfloat16 or wider, within the bound.
A program may use at most 192 MiB of HBM per device.

```python
import math
import jax
import jax.numpy as jnp
import numpy as np
from jax import lax

D_IN = 4096
PC = 1024
LISTS = 256
ROWS_DEV = 2048
MOST = 16
ROWS = 32768
N_DIM = 2
N_GRP = 16


def with_ends(drawn, key, smallest, high):
    shape = drawn.shape
    place = [jax.random.randint(jax.random.fold_in(key, axis), (), 0, shape[axis]) for axis in range(len(shape))]
    drawn = drawn.at[tuple(place)].set(smallest)
    longest = shape.index(max(shape))
    place[longest] = (place[longest] + 1) % shape[longest]
    return drawn.at[tuple(place)].set(high)


def strengthened(array, own_key, source, target, blocks, factor):
    owner, partner = [(jnp.arange(array.shape[position]) // (array.shape[position] // blocks)).reshape([-1 if axis == position else 1 for axis in range(array.ndim)]) for position in (source, target)]
    chosen = jax.random.permutation(own_key, blocks)[partner]
    strong = (owner == chosen) | (owner == (partner + blocks // 2) % blocks)
    return jnp.where(strong, factor * array, array)


def block_levels(own_key, extent, cuts, least, largest):
    factor_of, own = 1.0, jax.random.fold_in(own_key, 6)
    for dim, shards_of in cuts:
        draws = jnp.exp(jax.random.uniform(jax.random.fold_in(own, dim), (shards_of,), jnp.float32, least / len(cuts), largest / len(cuts)))
        factor_of = factor_of * jnp.repeat(draws, extent[dim] // shards_of).reshape([-1 if axis == dim else 1 for axis in range(len(extent))])
    return factor_of


def routed_block(stream_key, own, number, rows, amount, top, reach, slope):
    sequence = jax.random.permutation(stream_key, amount)
    packed, ordinary = portions_of(amount, rows * top, reach, slope, True), portions_of(amount, rows * top, reach, slope, False)
    places = jnp.arange(amount)

    def named(tallies, turn):
        used = int((tallies > 0).sum())
        fixed = max(1, used // 4)
        passed = fixed + (places - fixed + turn * (used - fixed)) % max(1, amount - fixed)
        return jnp.zeros((amount,), jnp.int32).at[sequence[jnp.where(places < fixed, places, passed)]].set(jnp.asarray(tallies, jnp.int32))

    tallies = jnp.where(number % 4 == 0, named(packed, number // 4), named(ordinary, number - number // 4 - 1))
    mixed = jax.random.permutation(jax.random.fold_in(own, 3), amount)
    source_of, receiver = mixed[0:amount // 2 * 2:2], mixed[1:amount // 2 * 2:2]
    slack = jnp.minimum(tallies[source_of] - 1, reach - tallies[receiver]) // 2
    slack = jnp.where((source_of == sequence[0]) | (receiver == sequence[0]) | (tallies[receiver] == 0), 0, jnp.maximum(slack, 0))
    passed = jax.random.randint(jax.random.fold_in(own, 4), (amount // 2,), 0, 1 << 20) % (slack + 1)
    tallies = tallies.at[source_of].add(-passed).at[receiver].add(passed)
    items = jnp.searchsorted(jnp.cumsum(tallies), jnp.arange(rows * top), side="right").astype(jnp.int32)
    table = items.reshape(top, rows).T
    table = table[jax.random.permutation(jax.random.fold_in(own, 1), rows)]
    turn = jax.random.randint(jax.random.fold_in(own, 2), (rows, 1), 0, top)
    return jnp.take_along_axis(table, (jnp.arange(top)[None, :] + turn) % top, axis=1)


def portions_of(count, total, most, lean, full):
    loads = [(1 << 20) // math.isqrt(standing ** lean) + 1 for standing in range(1, count + 1)]
    largest = most if full else min(most, max(-(-total // count), total * loads[0] // sum(loads)))
    least = 1 if total - largest >= count - 1 else 0
    holding, rest = [largest] + [least] * (count - 1), total - largest - least * (count - 1)
    while rest > 0:
        movable = [i for i in range(1, count) if holding[i] < largest] or [i for i in range(1, count) if holding[i] < most]
        pool, budget = sum([loads[i] for i in movable]), rest
        for i in movable:
            more = min(most - holding[i], max(1, budget * loads[i] // pool), rest)
            holding[i] = holding[i] + more
            rest = rest - more
    return np.array(holding)


def normal_values(own_key, shape, spread, limit, cuts=(), kind=jnp.bfloat16):
    result = jax.random.normal(own_key, shape, jnp.float32) * spread
    if len(cuts) > 0:
        result = block_levels(own_key, shape, cuts, -0.22, 0.18) * result
    return jnp.clip(result, min=-limit, max=limit).astype(kind)


def bell_draw_with(key, shape, scale, most, split, heavy, held_as=jnp.bfloat16):
    values = scale * jax.random.normal(key, shape, jnp.float32)
    if split:
        values = values * block_levels(key, shape, split, -0.22, 0.18)
    return jnp.clip(strengthened(values, jax.random.fold_in(key, 3), *heavy), -most, most).astype(held_as)


def setup_inputs(seed: int = 0) -> dict:
    key_list = jax.random.split(jax.random.key(seed), 7)
    states = normal_values(key_list[0], (ROWS, D_IN), 1.0, 6.0, ((0, 16), (1, 2)))
    pca = bell_draw_with(key_list[1], (D_IN, PC), D_IN ** -0.5, 0.125, ((0, 2),), (0, 1, 2, 2.0))
    centroids = normal_values(key_list[2], (LISTS, PC), 0.5, 3.0, ((1, 2),), jnp.float32)
    list_ids_keys = jax.random.split(jax.random.fold_in(key_list[3], 1), ROWS // ROWS_DEV)
    list_ids_turns = jax.random.permutation(jax.random.fold_in(key_list[3], 3), ROWS // ROWS_DEV)
    list_ids = jax.vmap(lambda own, number: routed_block(jax.random.fold_in(key_list[3], 2), own, number, ROWS_DEV, LISTS, 1, MOST, 2))(list_ids_keys, list_ids_turns).reshape((ROWS, 1))
    prior_counts = with_ends(jax.random.randint(key_list[4], (LISTS,), 1, 64), jax.random.fold_in(key_list[4], 1), 1, 63).astype(jnp.int32)
    prior_gram = normal_values(key_list[5], (LISTS, PC, PC), 16.0, 96.0, ((0, 16), (1, 2)), jnp.float32)
    return {"states": states, "pca": pca, "centroids": centroids, "list_ids": list_ids, "prior_counts": prior_counts, "prior_gram": prior_gram}


def outer_sum(block):
    return jnp.dot(block.T, block, preferred_element_type=jnp.float32)


def reference(states, pca, centroids, list_ids, prior_counts, prior_gram):
    width = D_IN // N_DIM
    total_rows = states.shape[0]
    projected = jnp.zeros((total_rows, PC), jnp.float32)
    for index in range(N_DIM):
        partial_sum = jnp.dot(states[:, index * width:(index + 1) * width], pca[index * width:(index + 1) * width], preferred_element_type=jnp.float32)
        rounded = lax.optimization_barrier(partial_sum.astype(jnp.bfloat16))
        projected = projected + rounded.astype(jnp.float32)
    labels = list_ids[:, 0].astype(jnp.int32)
    residual = (projected - centroids[labels]).astype(jnp.bfloat16)
    new_counts = jax.ops.segment_sum(jnp.ones((total_rows,), jnp.int32), labels, num_segments=LISTS).astype(jnp.int32)
    order = jnp.argsort(labels, stable=True).astype(jnp.int32)
    sorted_labels = labels[order]
    starts = (jnp.cumsum(new_counts) - new_counts).astype(jnp.int32)
    ranks = jnp.arange(total_rows, dtype=jnp.int32) - starts[sorted_labels]
    capacity = N_GRP * MOST
    padded = jnp.zeros((LISTS, capacity, PC), jnp.bfloat16).at[sorted_labels, ranks].set(residual[order])
    new_gram = lax.map(outer_sum, padded)
    totals = (prior_counts + new_counts).astype(jnp.float32)
    return (prior_gram + new_gram) / totals[:, None, None]
```

```python
import functools

import jax
import jax.numpy as jnp
from jax import lax
from jax.experimental import pallas as pl
from jax.experimental.pallas import tpu as pltpu
from jax.sharding import PartitionSpec as P

MOST = 16
BLOCK = 256
MESH = pl.DeviceIdType.MESH
CONTRACT_FIRST = (((0,), (0,)), ((), ()))


def route_kernel(
    n, states_hbm, pca_hbm, cent_ref, labels_ref, gath, counts_out,
    states, pca, pieces, to_peer, from_peer, residual, slots, packed, counts,
    states_sem, pca_sem, peer_send, peer_recv, send, recv, pass_send, pass_recv,
    count_send, count_recv, own_sem,
):
    dim, me = lax.axis_index("dim"), lax.axis_index("grp")
    other = 1 - dim
    rows, depth = states.shape
    width = residual.shape[1]
    lists = cent_ref.shape[0]
    cap = packed.shape[1]
    per = lists // n
    blocks = rows // BLOCK

    barrier = pltpu.get_barrier_semaphore()
    pl.semaphore_signal(barrier, inc=1, device_id={"dim": other}, device_id_type=MESH)

    @pl.loop(1, n)
    def _(j):
        pl.semaphore_signal(
            barrier, inc=1, device_id={"grp": lax.rem(me + j, n)}, device_id_type=MESH
        )

    pca_copy = pltpu.make_async_copy(pca_hbm, pca, pca_sem)
    pca_copy.start()

    def states_copy(b):
        at = pl.ds(b * BLOCK, BLOCK)
        return pltpu.make_async_copy(states_hbm.at[at], states.at[at], states_sem.at[b])

    @pl.loop(0, blocks)
    def _(b):
        states_copy(b).start()

    list_of = lax.broadcasted_iota(jnp.int32, (lists, BLOCK), 0)

    def named(b):
        return labels_ref[:, pl.ds(pl.multiple_of(b * BLOCK, BLOCK), BLOCK)] == list_of

    before = (
        lax.broadcasted_iota(jnp.int32, (BLOCK, BLOCK), 0)
        < lax.broadcasted_iota(jnp.int32, (BLOCK, BLOCK), 1)
    ).astype(jnp.float32).astype(jnp.bfloat16)

    def rank_step(b, seen):
        here = named(b)
        onehot = here.astype(jnp.float32)
        earlier = seen + jnp.dot(
            onehot.astype(jnp.bfloat16), before, preferred_element_type=jnp.float32
        )
        ranks = jnp.sum(onehot * earlier, axis=0, keepdims=True).astype(jnp.int32)
        at = pl.ds(pl.multiple_of(b * BLOCK, BLOCK), BLOCK)
        slots[:, at] = labels_ref[:, at] * MOST + ranks
        return seen + jnp.sum(onehot, axis=1, keepdims=True)

    seen = lax.fori_loop(0, blocks, rank_step, jnp.zeros((lists, 1), jnp.float32))
    tallies = jnp.broadcast_to(seen, (lists, 128)).astype(jnp.int32)
    for d in range(n):
        counts[d] = tallies[d * per : (d + 1) * per]

    cent = cent_ref[...]
    high = cent.astype(jnp.bfloat16)
    pieces[0] = high
    rest = cent - high.astype(jnp.float32)
    middle = rest.astype(jnp.bfloat16)
    pieces[1] = middle
    pieces[2] = (rest - middle.astype(jnp.float32)).astype(jnp.bfloat16)

    pl.semaphore_wait(barrier, n)
    pca_copy.wait()

    def peer_copy(b):
        at = pl.ds(pl.multiple_of(b * BLOCK, BLOCK), BLOCK)
        return pltpu.make_async_remote_copy(
            src_ref=to_peer.at[at], dst_ref=from_peer.at[at],
            send_sem=peer_send.at[b], recv_sem=peer_recv.at[b],
            device_id={"dim": other}, device_id_type=MESH,
        )

    def partial(b, part):
        at = pl.ds(pl.multiple_of(b * BLOCK, BLOCK), BLOCK)
        columns = pl.ds(pl.multiple_of(part * width, width), width)
        return jnp.dot(
            states[at, :], pca[:, columns], preferred_element_type=jnp.float32
        ).astype(jnp.bfloat16)

    @pl.loop(0, blocks)
    def _(b):
        states_copy(b).wait()
        to_peer[pl.ds(pl.multiple_of(b * BLOCK, BLOCK), BLOCK), :] = partial(b, other)
        peer_copy(b).start()

    @pl.loop(0, blocks)
    def _(b):
        at = pl.ds(pl.multiple_of(b * BLOCK, BLOCK), BLOCK)
        onehot = named(b).astype(jnp.float32).astype(jnp.bfloat16)
        shift = sum(
            lax.dot_general(
                onehot, pieces[i], CONTRACT_FIRST, preferred_element_type=jnp.float32
            )
            for i in (2, 1, 0)
        )
        own = partial(b, dim).astype(jnp.float32)
        peer_copy(b).wait_recv()
        projected = own + from_peer[at, :].astype(jnp.float32)
        residual[at, :] = (projected - shift).astype(jnp.bfloat16)

    def block_copy(d, source):
        return pltpu.make_async_remote_copy(
            src_ref=packed.at[d], dst_ref=gath.at[dim, source],
            send_sem=send.at[d], recv_sem=recv.at[source],
            device_id={"grp": d}, device_id_type=MESH,
        )

    def count_copy(d, source):
        return pltpu.make_async_remote_copy(
            src_ref=counts.at[d], dst_ref=counts_out.at[source],
            send_sem=count_send.at[d], recv_sem=count_recv.at[source],
            device_id={"grp": d}, device_id_type=MESH,
        )

    def pass_copy(source, half):
        return pltpu.make_async_remote_copy(
            src_ref=gath.at[half, source], dst_ref=gath.at[half, source],
            send_sem=pass_send.at[source], recv_sem=pass_recv.at[source],
            device_id={"dim": other}, device_id_type=MESH,
        )

    slot_of = lax.broadcasted_iota(jnp.int32, (cap, rows), 0)

    @pl.loop(0, n)
    def _(j):
        d = lax.rem(me + n // 2 + j, n)
        chosen = (slots[...] - d * cap == slot_of).astype(jnp.float32).astype(jnp.bfloat16)
        packed[d] = jnp.dot(
            chosen, residual[...], preferred_element_type=jnp.float32
        ).astype(jnp.bfloat16)

        @pl.when(j != n // 2)
        def _():
            block_copy(d, me).start()
            count_copy(d, me).start()

    own_block = pltpu.make_async_copy(packed.at[me], gath.at[dim, me], own_sem.at[0])
    own_count = pltpu.make_async_copy(counts.at[me], counts_out.at[me], own_sem.at[1])
    own_block.start()
    own_count.start()
    own_block.wait()
    own_count.wait()
    pass_copy(me, dim).start()

    @pl.loop(0, n)
    def _(j):
        source = lax.rem(me + n + n // 2 - j, n)

        @pl.when(j != n // 2)
        def _():
            block_copy(source, source).wait_recv()
            pass_copy(source, dim).start()
            count_copy(source, source).wait_recv()

    @pl.loop(0, n)
    def _(j):
        pass_copy(j, dim).wait_send()
        pass_copy(j, other).wait_recv()

    @pl.loop(1, n)
    def _(j):
        d = lax.rem(me + j, n)
        block_copy(d, me).wait_send()
        count_copy(d, me).wait_send()

    @pl.loop(0, blocks)
    def _(b):
        peer_copy(b).wait_send()


def moment_kernel(prior_counts_ref, counts_ref, rows_ref, prior_ref, out_ref):
    dim = lax.axis_index("dim")
    l = pl.program_id(0)
    halves, n, most, width = rows_ref.shape
    total = prior_counts_ref[l] + jnp.sum(counts_ref[:, pl.ds(l, 1), :], axis=0)
    inverse = 1.0 / total.astype(jnp.float32)
    own = rows_ref[dim].reshape(n * most, width)
    for half in range(halves):
        columns = pl.ds(half * width, width)
        gram = lax.dot_general(
            own, rows_ref[half].reshape(n * most, width), CONTRACT_FIRST,
            preferred_element_type=jnp.float32,
        )
        out_ref[0, :, columns] = (prior_ref[0, :, columns] + gram) * inverse[:, :1]


def on_device(n, states, pca, centroids, list_ids, prior_counts, prior_gram):
    rows, depth = states.shape
    lists, width = centroids.shape
    per = lists // n
    cap = per * MOST
    blocks = rows // BLOCK
    dma = pltpu.SemaphoreType.DMA
    vmem = pltpu.VMEM
    any_space = pl.BlockSpec(memory_space=pl.ANY)
    gathered, counts = pl.pallas_call(
        functools.partial(route_kernel, n),
        out_shape=(
            jax.ShapeDtypeStruct((2, n, cap, width), jnp.bfloat16),
            jax.ShapeDtypeStruct((n, per, 128), jnp.int32),
        ),
        in_specs=[
            any_space,
            any_space,
            pl.BlockSpec(memory_space=vmem),
            pl.BlockSpec(memory_space=vmem),
        ],
        out_specs=(any_space, any_space),
        scratch_shapes=[
            vmem((rows, depth), jnp.bfloat16),
            vmem(pca.shape, jnp.bfloat16),
            vmem((3, lists, width), jnp.bfloat16),
            vmem((rows, width), jnp.bfloat16),
            vmem((rows, width), jnp.bfloat16),
            vmem((rows, width), jnp.bfloat16),
            vmem((1, rows), jnp.int32),
            vmem((n, cap, width), jnp.bfloat16),
            vmem((n, per, 128), jnp.int32),
            dma((blocks,)), dma, dma((blocks,)), dma((blocks,)),
            dma((n,)), dma((n,)), dma((n,)), dma((n,)), dma((n,)), dma((n,)), dma((2,)),
        ],
        compiler_params=pltpu.CompilerParams(
            collective_id=0, has_side_effects=True, vmem_limit_bytes=44 * 2**20
        ),
        name="route",
    )(states, pca, centroids, list_ids.reshape(1, rows))
    own = prior_gram.shape[1]
    gram_block = pl.BlockSpec((1, own, 2 * width), lambda l: (l, 0, 0))
    return pl.pallas_call(
        moment_kernel,
        grid=(per,),
        out_shape=jax.ShapeDtypeStruct(prior_gram.shape, jnp.float32),
        in_specs=[
            pl.BlockSpec(memory_space=pltpu.SMEM),
            pl.BlockSpec((n, per, 128), lambda l: (0, 0, 0)),
            pl.BlockSpec((2, n, MOST, width), lambda l: (0, 0, l, 0)),
            gram_block,
        ],
        out_specs=gram_block,
        compiler_params=pltpu.CompilerParams(vmem_limit_bytes=44 * 2**20),
        name="moments",
    )(prior_counts, counts, gathered, prior_gram)


def solution(mesh):
    in_specs = (
        P("grp", "dim"),
        P("dim", None),
        P(None, "dim"),
        P("grp", None),
        P("grp"),
        P("grp", "dim", None),
    )
    return jax.shard_map(
        functools.partial(on_device, mesh.shape["grp"]),
        mesh=mesh,
        in_specs=in_specs,
        out_specs=P("grp", "dim", None),
        check_vma=False,
    )
```

```python
import functools

import jax
import jax.numpy as jnp
from jax import lax
from jax.experimental import pallas as pl
from jax.experimental.pallas import tpu as pltpu
from jax.sharding import PartitionSpec as P

MOST = 16
BLOCK = 256
PARTS = 2
MESH = pl.DeviceIdType.MESH
CONTRACT_FIRST = (((0,), (0,)), ((), ()))


def route_kernel(
    n, states_hbm, pca_hbm, cent_ref, labels_ref, gath, counts_out,
    states, pca, pieces, to_peer, from_peer, residual, slots, packed, counts,
    states_sem, pca_sem, peer_send, peer_recv, send, recv, pass_send, pass_recv,
    count_send, count_recv, own_sem,
):
    dim, me = lax.axis_index("dim"), lax.axis_index("grp")
    other = 1 - dim
    rows, depth = states.shape
    part = residual.shape[2]
    lists = cent_ref.shape[0]
    cap = packed.shape[2]
    per = lists // n
    blocks = rows // BLOCK

    barrier = pltpu.get_barrier_semaphore()
    pl.semaphore_signal(barrier, inc=1, device_id={"dim": other}, device_id_type=MESH)

    @pl.loop(1, n)
    def _(j):
        pl.semaphore_signal(
            barrier, inc=1, device_id={"grp": lax.rem(me + j, n)}, device_id_type=MESH
        )

    pca_copy = pltpu.make_async_copy(pca_hbm, pca, pca_sem)
    pca_copy.start()

    def states_copy(b):
        at = pl.ds(b * BLOCK, BLOCK)
        return pltpu.make_async_copy(states_hbm.at[at], states.at[at], states_sem.at[b])

    @pl.loop(0, blocks)
    def _(b):
        states_copy(b).start()

    list_of = lax.broadcasted_iota(jnp.int32, (lists, BLOCK), 0)

    def named(b):
        return labels_ref[:, pl.ds(pl.multiple_of(b * BLOCK, BLOCK), BLOCK)] == list_of

    before = (
        lax.broadcasted_iota(jnp.int32, (BLOCK, BLOCK), 0)
        < lax.broadcasted_iota(jnp.int32, (BLOCK, BLOCK), 1)
    ).astype(jnp.float32).astype(jnp.bfloat16)

    def rank_step(b, seen):
        here = named(b)
        onehot = here.astype(jnp.float32)
        earlier = seen + jnp.dot(
            onehot.astype(jnp.bfloat16), before, preferred_element_type=jnp.float32
        )
        ranks = jnp.sum(onehot * earlier, axis=0, keepdims=True).astype(jnp.int32)
        at = pl.ds(pl.multiple_of(b * BLOCK, BLOCK), BLOCK)
        slots[:, at] = labels_ref[:, at] * MOST + ranks
        return seen + jnp.sum(onehot, axis=1, keepdims=True)

    seen = lax.fori_loop(0, blocks, rank_step, jnp.zeros((lists, 1), jnp.float32))
    tallies = jnp.broadcast_to(seen, (lists, 128)).astype(jnp.int32)
    for d in range(n):
        counts[d] = tallies[d * per : (d + 1) * per]

    cent = cent_ref[...]
    high = cent.astype(jnp.bfloat16)
    pieces[0] = high
    rest = cent - high.astype(jnp.float32)
    middle = rest.astype(jnp.bfloat16)
    pieces[1] = middle
    pieces[2] = (rest - middle.astype(jnp.float32)).astype(jnp.bfloat16)

    pl.semaphore_wait(barrier, n)
    pca_copy.wait()

    def rows_at(b):
        return pl.ds(pl.multiple_of(b * BLOCK, BLOCK), BLOCK)

    def peer_copy(q, b):
        return pltpu.make_async_remote_copy(
            src_ref=to_peer.at[q, rows_at(b)], dst_ref=from_peer.at[q, rows_at(b)],
            send_sem=peer_send.at[q * blocks + b], recv_sem=peer_recv.at[q * blocks + b],
            device_id={"dim": other}, device_id_type=MESH,
        )

    def partial(q, b, owner):
        columns = pl.ds(pl.multiple_of((owner * PARTS + q) * part, part), part)
        return jnp.dot(
            states[rows_at(b), :], pca[:, columns], preferred_element_type=jnp.float32
        ).astype(jnp.bfloat16)

    def block_copy(q, d, source):
        return pltpu.make_async_remote_copy(
            src_ref=packed.at[q, d], dst_ref=gath.at[dim * PARTS + q, source],
            send_sem=send.at[q * n + d], recv_sem=recv.at[q * n + source],
            device_id={"grp": d}, device_id_type=MESH,
        )

    def count_copy(d, source):
        return pltpu.make_async_remote_copy(
            src_ref=counts.at[d], dst_ref=counts_out.at[source],
            send_sem=count_send.at[d], recv_sem=count_recv.at[source],
            device_id={"grp": d}, device_id_type=MESH,
        )

    def pass_copy(q, source, half):
        return pltpu.make_async_remote_copy(
            src_ref=gath.at[half * PARTS + q, source], dst_ref=gath.at[half * PARTS + q, source],
            send_sem=pass_send.at[q * n + source], recv_sem=pass_recv.at[q * n + source],
            device_id={"dim": other}, device_id_type=MESH,
        )

    def own_copy(q):
        return pltpu.make_async_copy(
            packed.at[q, me], gath.at[dim * PARTS + q, me], own_sem.at[q]
        )

    own_count = pltpu.make_async_copy(counts.at[me], counts_out.at[me], own_sem.at[PARTS])
    own_count.start()
    slot_of = lax.broadcasted_iota(jnp.int32, (cap, rows), 0)

    for q in range(PARTS):

        @pl.loop(0, blocks)
        def _(b):
            if q == 0:
                states_copy(b).wait()
            to_peer[q, rows_at(b), :] = partial(q, b, other)
            peer_copy(q, b).start()

        @pl.loop(0, blocks)
        def _(b):
            onehot = named(b).astype(jnp.float32).astype(jnp.bfloat16)
            shift = sum(
                lax.dot_general(
                    onehot, pieces[i, :, q * part : (q + 1) * part], CONTRACT_FIRST,
                    preferred_element_type=jnp.float32,
                )
                for i in (2, 1, 0)
            )
            own = partial(q, b, dim).astype(jnp.float32)
            peer_copy(q, b).wait_recv()
            projected = own + from_peer[q, rows_at(b), :].astype(jnp.float32)
            residual[q, rows_at(b), :] = (projected - shift).astype(jnp.bfloat16)

        @pl.loop(0, n)
        def _(j):
            d = lax.rem(me + n // 2 + j, n)
            chosen = (slots[...] - d * cap == slot_of).astype(jnp.float32).astype(jnp.bfloat16)
            packed[q, d] = jnp.dot(
                chosen, residual[q], preferred_element_type=jnp.float32
            ).astype(jnp.bfloat16)

            @pl.when(j != n // 2)
            def _():
                block_copy(q, d, me).start()
                if q == 0:
                    count_copy(d, me).start()

        own_copy(q).start()

    for q in range(PARTS):
        own_copy(q).wait()
        pass_copy(q, me, dim).start()

        @pl.loop(0, n)
        def _(j):
            source = lax.rem(me + n + n // 2 - j, n)

            @pl.when(j != n // 2)
            def _():
                block_copy(q, source, source).wait_recv()
                pass_copy(q, source, dim).start()

    own_count.wait()

    @pl.loop(1, n)
    def _(j):
        d = lax.rem(me + j, n)
        count_copy(d, d).wait_recv()
        count_copy(d, me).wait_send()

    for q in range(PARTS):

        @pl.loop(0, n)
        def _(j):
            pass_copy(q, j, dim).wait_send()
            pass_copy(q, j, other).wait_recv()

        @pl.loop(1, n)
        def _(j):
            block_copy(q, lax.rem(me + j, n), me).wait_send()

        @pl.loop(0, blocks)
        def _(b):
            peer_copy(q, b).wait_send()


def moment_kernel(prior_counts_ref, counts_ref, rows_ref, prior_ref, out_ref):
    dim = lax.axis_index("dim")
    l = pl.program_id(0)
    pieces, n, most, part = rows_ref.shape
    total = prior_counts_ref[l] + jnp.sum(counts_ref[:, pl.ds(l, 1), :], axis=0)
    inverse = 1.0 / total.astype(jnp.float32)
    own = jnp.concatenate(
        [rows_ref[dim * PARTS + q].reshape(n * most, part) for q in range(PARTS)], axis=1
    )
    for piece in range(pieces):
        columns = pl.ds(piece * part, part)
        gram = lax.dot_general(
            own, rows_ref[piece].reshape(n * most, part), CONTRACT_FIRST,
            preferred_element_type=jnp.float32,
        )
        out_ref[0, :, columns] = (prior_ref[0, :, columns] + gram) * inverse[:, :1]


def on_device(n, states, pca, centroids, list_ids, prior_counts, prior_gram):
    rows, depth = states.shape
    lists, width = centroids.shape
    per = lists // n
    cap = per * MOST
    blocks = rows // BLOCK
    part = width // PARTS
    dma = pltpu.SemaphoreType.DMA
    vmem = pltpu.VMEM
    any_space = pl.BlockSpec(memory_space=pl.ANY)
    gathered, counts = pl.pallas_call(
        functools.partial(route_kernel, n),
        out_shape=(
            jax.ShapeDtypeStruct((2 * PARTS, n, cap, part), jnp.bfloat16),
            jax.ShapeDtypeStruct((n, per, 128), jnp.int32),
        ),
        in_specs=[
            any_space,
            any_space,
            pl.BlockSpec(memory_space=vmem),
            pl.BlockSpec(memory_space=vmem),
        ],
        out_specs=(any_space, any_space),
        scratch_shapes=[
            vmem((rows, depth), jnp.bfloat16),
            vmem(pca.shape, jnp.bfloat16),
            vmem((3, lists, width), jnp.bfloat16),
            vmem((PARTS, rows, part), jnp.bfloat16),
            vmem((PARTS, rows, part), jnp.bfloat16),
            vmem((PARTS, rows, part), jnp.bfloat16),
            vmem((1, rows), jnp.int32),
            vmem((PARTS, n, cap, part), jnp.bfloat16),
            vmem((n, per, 128), jnp.int32),
            dma((blocks,)), dma, dma((PARTS * blocks,)), dma((PARTS * blocks,)),
            dma((PARTS * n,)), dma((PARTS * n,)), dma((PARTS * n,)), dma((PARTS * n,)),
            dma((n,)), dma((n,)), dma((PARTS + 1,)),
        ],
        compiler_params=pltpu.CompilerParams(
            collective_id=0, has_side_effects=True, vmem_limit_bytes=60 * 2**20
        ),
        name="route",
    )(states, pca, centroids, list_ids.reshape(1, rows))
    own = prior_gram.shape[1]
    gram_block = pl.BlockSpec((1, own, 2 * width), lambda l: (l, 0, 0))
    return pl.pallas_call(
        moment_kernel,
        grid=(per,),
        out_shape=jax.ShapeDtypeStruct(prior_gram.shape, jnp.float32),
        in_specs=[
            pl.BlockSpec(memory_space=pltpu.SMEM),
            pl.BlockSpec((n, per, 128), lambda l: (0, 0, 0)),
            pl.BlockSpec((2 * PARTS, n, MOST, part), lambda l: (0, 0, l, 0)),
            gram_block,
        ],
        out_specs=gram_block,
        compiler_params=pltpu.CompilerParams(vmem_limit_bytes=60 * 2**20),
        name="moments",
    )(prior_counts, counts, gathered, prior_gram)


def solution(mesh):
    in_specs = (
        P("grp", "dim"),
        P("dim", None),
        P(None, "dim"),
        P("grp", None),
        P("grp"),
        P("grp", "dim", None),
    )
    return jax.shard_map(
        functools.partial(on_device, mesh.shape["grp"]),
        mesh=mesh,
        in_specs=in_specs,
        out_specs=P("grp", "dim", None),
        check_vma=False,
    )
```

```python
import functools

import jax
import jax.numpy as jnp
from jax import lax
from jax.experimental import pallas as pl
from jax.experimental.pallas import tpu as pltpu
from jax.sharding import PartitionSpec as P

MOST = 16
BLOCK = 256
PARTS = 2
MESH = pl.DeviceIdType.MESH
CONTRACT_FIRST = (((0,), (0,)), ((), ()))


def route_kernel(
    n, states_hbm, pca_hbm, cent_ref, labels_ref, gath, counts_out,
    states, pca, pieces, to_peer, from_peer, residual, slots, packed, counts,
    states_sem, pca_sem, peer_send, peer_recv, send, recv, pass_send, pass_recv,
    count_send, count_recv, own_sem,
):
    dim, me = lax.axis_index("dim"), lax.axis_index("grp")
    other = 1 - dim
    rows, depth = states.shape
    part = residual.shape[2]
    lists = cent_ref.shape[0]
    cap = packed.shape[2]
    per = lists // n
    blocks = rows // BLOCK

    barrier = pltpu.get_barrier_semaphore()
    pl.semaphore_signal(barrier, inc=1, device_id={"dim": other}, device_id_type=MESH)

    @pl.loop(1, n)
    def _(j):
        pl.semaphore_signal(
            barrier, inc=1, device_id={"grp": lax.rem(me + j, n)}, device_id_type=MESH
        )

    pca_copy = pltpu.make_async_copy(pca_hbm, pca, pca_sem)
    pca_copy.start()

    def states_copy(b):
        at = pl.ds(b * BLOCK, BLOCK)
        return pltpu.make_async_copy(states_hbm.at[at], states.at[at], states_sem.at[b])

    @pl.loop(0, blocks)
    def _(b):
        states_copy(b).start()

    list_of = lax.broadcasted_iota(jnp.int32, (lists, BLOCK), 0)

    def named(b):
        return labels_ref[:, pl.ds(pl.multiple_of(b * BLOCK, BLOCK), BLOCK)] == list_of

    before = (
        lax.broadcasted_iota(jnp.int32, (BLOCK, BLOCK), 0)
        < lax.broadcasted_iota(jnp.int32, (BLOCK, BLOCK), 1)
    ).astype(jnp.float32).astype(jnp.bfloat16)

    def rank_step(b, seen):
        here = named(b)
        onehot = here.astype(jnp.float32)
        earlier = seen + jnp.dot(
            onehot.astype(jnp.bfloat16), before, preferred_element_type=jnp.float32
        )
        ranks = jnp.sum(onehot * earlier, axis=0, keepdims=True).astype(jnp.int32)
        at = pl.ds(pl.multiple_of(b * BLOCK, BLOCK), BLOCK)
        slots[:, at] = labels_ref[:, at] * MOST + ranks
        return seen + jnp.sum(onehot, axis=1, keepdims=True)

    seen = lax.fori_loop(0, blocks, rank_step, jnp.zeros((lists, 1), jnp.float32))
    tallies = jnp.broadcast_to(seen, (lists, 128)).astype(jnp.int32)
    for d in range(n):
        counts[d] = tallies[d * per : (d + 1) * per]

    cent = cent_ref[...]
    high = cent.astype(jnp.bfloat16)
    pieces[0] = high
    rest = cent - high.astype(jnp.float32)
    middle = rest.astype(jnp.bfloat16)
    pieces[1] = middle
    pieces[2] = (rest - middle.astype(jnp.float32)).astype(jnp.bfloat16)

    pl.semaphore_wait(barrier, n)
    pca_copy.wait()

    def rows_at(b):
        return pl.ds(pl.multiple_of(b * BLOCK, BLOCK), BLOCK)

    def peer_copy(q, b):
        return pltpu.make_async_remote_copy(
            src_ref=to_peer.at[q, rows_at(b)], dst_ref=from_peer.at[q, rows_at(b)],
            send_sem=peer_send.at[q * blocks + b], recv_sem=peer_recv.at[q * blocks + b],
            device_id={"dim": other}, device_id_type=MESH,
        )

    def partial(q, b, owner):
        columns = pl.ds(pl.multiple_of((owner * PARTS + q) * part, part), part)
        return jnp.dot(
            states[rows_at(b), :], pca[:, columns], preferred_element_type=jnp.float32
        ).astype(jnp.bfloat16)

    def block_copy(q, d, source):
        return pltpu.make_async_remote_copy(
            src_ref=packed.at[q, d], dst_ref=gath.at[dim * PARTS + q, source],
            send_sem=send.at[q * n + d], recv_sem=recv.at[q * n + source],
            device_id={"grp": d}, device_id_type=MESH,
        )

    def count_copy(d, source):
        return pltpu.make_async_remote_copy(
            src_ref=counts.at[d], dst_ref=counts_out.at[source],
            send_sem=count_send.at[d], recv_sem=count_recv.at[source],
            device_id={"grp": d}, device_id_type=MESH,
        )

    def pass_copy(q, source, half):
        return pltpu.make_async_remote_copy(
            src_ref=gath.at[half * PARTS + q, source], dst_ref=gath.at[half * PARTS + q, source],
            send_sem=pass_send.at[q * n + source], recv_sem=pass_recv.at[q * n + source],
            device_id={"dim": other}, device_id_type=MESH,
        )

    def own_copy(q):
        return pltpu.make_async_copy(
            packed.at[q, me], gath.at[dim * PARTS + q, me], own_sem.at[q]
        )

    own_count = pltpu.make_async_copy(counts.at[me], counts_out.at[me], own_sem.at[PARTS])
    own_count.start()
    slot_of = lax.broadcasted_iota(jnp.int32, (cap, rows), 0)

    for q in range(PARTS):

        @pl.loop(0, blocks)
        def _(b):
            if q == 0:
                states_copy(b).wait()
            to_peer[q, rows_at(b), :] = partial(q, b, other)
            peer_copy(q, b).start()

        @pl.loop(0, blocks)
        def _(b):
            onehot = named(b).astype(jnp.float32).astype(jnp.bfloat16)
            shift = sum(
                lax.dot_general(
                    onehot, pieces[i, :, q * part : (q + 1) * part], CONTRACT_FIRST,
                    preferred_element_type=jnp.float32,
                )
                for i in (2, 1, 0)
            )
            own = partial(q, b, dim).astype(jnp.float32)
            peer_copy(q, b).wait_recv()
            projected = own + from_peer[q, rows_at(b), :].astype(jnp.float32)
            residual[q, rows_at(b), :] = (projected - shift).astype(jnp.bfloat16)

        @pl.loop(0, n)
        def _(j):
            d = lax.rem(me + n // 2 + j, n)
            chosen = (slots[...] - d * cap == slot_of).astype(jnp.float32).astype(jnp.bfloat16)
            packed[q, d] = jnp.dot(
                chosen, residual[q], preferred_element_type=jnp.float32
            ).astype(jnp.bfloat16)

            @pl.when(j != n // 2)
            def _():
                block_copy(q, d, me).start()
                if q == 0:
                    count_copy(d, me).start()

        own_copy(q).start()

    for q in range(PARTS):
        own_copy(q).wait()
        pass_copy(q, me, dim).start()

        @pl.loop(0, n)
        def _(j):
            source = lax.rem(me + n + n // 2 - j, n)

            @pl.when(j != n // 2)
            def _():
                block_copy(q, source, source).wait_recv()
                pass_copy(q, source, dim).start()

    own_count.wait()

    @pl.loop(1, n)
    def _(j):
        d = lax.rem(me + j, n)
        count_copy(d, d).wait_recv()
        count_copy(d, me).wait_send()

    for q in range(PARTS):

        @pl.loop(0, n)
        def _(j):
            pass_copy(q, j, dim).wait_send()
            pass_copy(q, j, other).wait_recv()

        @pl.loop(1, n)
        def _(j):
            block_copy(q, lax.rem(me + j, n), me).wait_send()

        @pl.loop(0, blocks)
        def _(b):
            peer_copy(q, b).wait_send()


def moment_kernel(prior_counts_ref, counts_ref, rows_ref, prior_ref, out_ref):
    dim = lax.axis_index("dim")
    l = pl.program_id(0)
    pieces, n, most, part = rows_ref.shape
    total = prior_counts_ref[l] + jnp.sum(counts_ref[:, pl.ds(l, 1), :], axis=0)
    inverse = 1.0 / total.astype(jnp.float32)
    own = jnp.concatenate(
        [rows_ref[dim * PARTS + q].reshape(n * most, part).T for q in range(PARTS)], axis=0
    )
    for piece in range(pieces):
        columns = pl.ds(piece * part, part)
        gram = jnp.dot(
            own, rows_ref[piece].reshape(n * most, part), preferred_element_type=jnp.float32
        )
        out_ref[0, :, columns] = (prior_ref[0, :, columns] + gram) * inverse[:, :1]


def on_device(n, states, pca, centroids, list_ids, prior_counts, prior_gram):
    rows, depth = states.shape
    lists, width = centroids.shape
    per = lists // n
    cap = per * MOST
    blocks = rows // BLOCK
    part = width // PARTS
    dma = pltpu.SemaphoreType.DMA
    vmem = pltpu.VMEM
    any_space = pl.BlockSpec(memory_space=pl.ANY)
    gathered, counts = pl.pallas_call(
        functools.partial(route_kernel, n),
        out_shape=(
            jax.ShapeDtypeStruct((2 * PARTS, n, cap, part), jnp.bfloat16),
            jax.ShapeDtypeStruct((n, per, 128), jnp.int32),
        ),
        in_specs=[
            any_space,
            any_space,
            pl.BlockSpec(memory_space=vmem),
            pl.BlockSpec(memory_space=vmem),
        ],
        out_specs=(any_space, any_space),
        scratch_shapes=[
            vmem((rows, depth), jnp.bfloat16),
            vmem(pca.shape, jnp.bfloat16),
            vmem((3, lists, width), jnp.bfloat16),
            vmem((PARTS, rows, part), jnp.bfloat16),
            vmem((PARTS, rows, part), jnp.bfloat16),
            vmem((PARTS, rows, part), jnp.bfloat16),
            vmem((1, rows), jnp.int32),
            vmem((PARTS, n, cap, part), jnp.bfloat16),
            vmem((n, per, 128), jnp.int32),
            dma((blocks,)), dma, dma((PARTS * blocks,)), dma((PARTS * blocks,)),
            dma((PARTS * n,)), dma((PARTS * n,)), dma((PARTS * n,)), dma((PARTS * n,)),
            dma((n,)), dma((n,)), dma((PARTS + 1,)),
        ],
        compiler_params=pltpu.CompilerParams(
            collective_id=0, has_side_effects=True, vmem_limit_bytes=60 * 2**20
        ),
        name="route",
    )(states, pca, centroids, list_ids.reshape(1, rows))
    own = prior_gram.shape[1]
    gram_block = pl.BlockSpec((1, own, 2 * width), lambda l: (l, 0, 0))
    return pl.pallas_call(
        moment_kernel,
        grid=(per,),
        out_shape=jax.ShapeDtypeStruct(prior_gram.shape, jnp.float32),
        in_specs=[
            pl.BlockSpec(memory_space=pltpu.SMEM),
            pl.BlockSpec((n, per, 128), lambda l: (0, 0, 0)),
            pl.BlockSpec((2 * PARTS, n, MOST, part), lambda l: (0, 0, l, 0)),
            gram_block,
        ],
        out_specs=gram_block,
        compiler_params=pltpu.CompilerParams(vmem_limit_bytes=60 * 2**20),
        name="moments",
    )(prior_counts, counts, gathered, prior_gram)


def solution(mesh):
    in_specs = (
        P("grp", "dim"),
        P("dim", None),
        P(None, "dim"),
        P("grp", None),
        P("grp"),
        P("grp", "dim", None),
    )
    return jax.shard_map(
        functools.partial(on_device, mesh.shape["grp"]),
        mesh=mesh,
        in_specs=in_specs,
        out_specs=P("grp", "dim", None),
        check_vma=False,
    )
```
